32 devices in a mesh: region: 4 (over z), sub: 8 (over y, x, core).
Axes of the slice: x: 2, y: 2, z: 4, core: 2. Of those that a mesh axis runs over, the one named last changes fastest.
Arguments:
- test_vectors: float32 [16, 131072], P(None, ('region', 'sub')), may hold values from -12 to 12
- weights: bfloat16 [1024, 8, 128, 128], P(('region', 'sub')), may hold values from 0.099609375 to 1
- block_cols: int32 [1024, 8], P(('region', 'sub')), may hold values from 0 to 127, as said below
- block_count: int32 [1024], P(('region', 'sub')), may hold values from 5 to 8, as said below
- halo_send: int32 [32, 4, 16], P(('region', 'sub')), may hold values from 0 to 31
- far_send: int32 [32, 8, 4], P(('region', 'sub')), may hold values from 0 to 31
Outputs:
- smoothed: bfloat16 [16, 131072], P(None, ('region', 'sub'))
- affinity: bfloat16 [1024, 8, 128, 128], P(('region', 'sub'))
The draws below stay inside these ranges and needn't reach their ends.
Inputs may be any that keep to these rules, and one draw needn't show every extreme that they name: `block_cols`: every table position is named by some live slot of its device's block rows. `block_count`: live slots of a block row come first.
All inputs are finite; a program needn't handle non-finite values.
Results may differ from the reference program's by a relative error of at most 0.0055.
Values may be sent and summed in bfloat16 or wider, within the bound.
A program may use at most 64 MiB of HBM per device.

```python
import jax
import jax.numpy as jnp
from jax import lax

BLK_DEV = 32
BLOCK = 128
VECS = 16
SLOTS = 8
SWEEPS = 3
HALO_BLK = 16
FAR_BLK = 4
TABLE = 128
NBLK = 1024
NODES = 131072
N_REGION = 4
N_SUB = 8


def draw_test_vectors(key, part):
    key = jax.random.fold_in(key, 13)
    ramp = 1.0 + 2.0 * jnp.arange(NODES, dtype=jnp.float32) / (NODES - 1)
    values = jnp.clip(jax.random.normal(key, (VECS, NODES), jnp.float32), -4.0, 4.0) * ramp
    return values.astype(jnp.float32)


def draw_block_cols(key, part):
    key = jax.random.fold_in(key, 11)
    front = 5 * BLK_DEV

    def one_device(dev_key):
        key_order, key_fill, key_rest = jax.random.split(dev_key, 3)
        order = jax.random.permutation(key_order, front)
        filler = jax.random.randint(key_fill, (front,), 0, TABLE)
        base = jnp.arange(front, dtype=jnp.int32)
        values = jnp.where(base < TABLE, base, filler)
        placed = values[jnp.argsort(order)]
        rest = jax.random.randint(key_rest, (BLK_DEV, SLOTS - 5), 0, TABLE)
        return jnp.concatenate([placed.reshape(BLK_DEV, 5), rest], axis=1)
    dev_keys = jax.vmap(lambda index: jax.random.fold_in(key, index))(jnp.arange(N_REGION * N_SUB))
    return jax.vmap(one_device)(dev_keys).reshape(NBLK, SLOTS).astype(jnp.int32)


def draw_block_count(key, part):
    key = jax.random.fold_in(key, 12)
    extra = jax.random.randint(key, (NBLK,), 0, 4)
    rows = jnp.arange(NBLK, dtype=jnp.int32)
    device_ids = rows // BLK_DEV
    counts = 5 + jnp.minimum(extra, device_ids % 4)
    in_block = rows % BLK_DEV
    counts = jnp.where(in_block == 0, SLOTS, jnp.where(in_block == 1, 5, counts))
    return counts.astype(jnp.int32)


def place_ends(values, own_key, smallest, high):
    longest = values.shape.index(max(values.shape))
    spots = []
    for shift in (0, 1):
        where = [jax.random.randint(jax.random.fold_in(own_key, axis), (), 0, length) for axis, length in enumerate(values.shape)]
        where[longest] = (where[longest] + shift) % values.shape[longest]
        spots.append(tuple(where))
    return values.at[spots[0]].set(smallest).at[spots[1]].set(high)


def steps_of(rng, extent, cuts, smallest, top_value):
    def one(axis_at, parts):
        draws = jax.random.uniform(jax.random.fold_in(jax.random.fold_in(rng, 6), axis_at), (parts,), jnp.float32, smallest / len(cuts), top_value / len(cuts))
        return jnp.repeat(jnp.exp(draws), extent[axis_at] // parts).reshape((-1,) + (1,) * (len(extent) - axis_at - 1))

    level = one(*cuts[0])
    for cut in cuts[1:]:
        level = level * one(*cut)
    return level


def setup_inputs(seed: int = 0) -> dict:
    key_of = jax.random.split(jax.random.key(seed), 7)
    return {
        "test_vectors": draw_test_vectors(jax.random.fold_in(key_of[6], 71), 0),
        "weights": jnp.clip(0.099609375 + 0.9003906 * jax.random.uniform(key_of[1], (NBLK, SLOTS, BLOCK, BLOCK), jnp.float32) ** steps_of(key_of[1], (NBLK, SLOTS, BLOCK, BLOCK), ((0, 32),), -0.2, 0.2), 0.099609375, 1.0).astype(jnp.bfloat16),
        "block_cols": draw_block_cols(jax.random.fold_in(key_of[6], 71), 0),
        "block_count": draw_block_count(jax.random.fold_in(key_of[6], 71), 0),
        "halo_send": place_ends(jax.random.randint(key_of[4], (N_REGION * N_SUB, 4, HALO_BLK), 0, BLK_DEV), jax.random.fold_in(key_of[4], 1), 0, BLK_DEV - 1).astype(jnp.int32),
        "far_send": place_ends(jax.random.randint(key_of[5], (N_REGION * N_SUB, N_SUB, FAR_BLK), 0, BLK_DEV), jax.random.fold_in(key_of[5], 1), 0, BLK_DEV - 1).astype(jnp.int32),
    }


damping = 2.0 / 3.0

def pick_rows(blocks, indices):
    return jax.vmap(lambda held, where_to: held[where_to])(blocks, indices)

def build_table(blocks, halo_send, far_send):
    dev_count = N_REGION * N_SUB
    outgoing = pick_rows(blocks, halo_send).reshape(N_REGION, N_SUB, 4, HALO_BLK, VECS, BLOCK)
    sub_low = jnp.roll(outgoing[:, :, 0], 1, axis=1)
    sub_high = jnp.roll(outgoing[:, :, 1], -1, axis=1)
    region_low = jnp.roll(outgoing[:, :, 2], 1, axis=0)
    region_high = jnp.roll(outgoing[:, :, 3], -1, axis=0)
    far_blocks = pick_rows(blocks, far_send).reshape(N_REGION, N_SUB, N_SUB, FAR_BLK, VECS, BLOCK)
    far_blocks = far_blocks.transpose(0, 2, 1, 3, 4, 5).reshape(N_REGION, N_SUB, N_SUB * FAR_BLK, VECS, BLOCK)
    own_blocks = blocks.reshape(N_REGION, N_SUB, BLK_DEV, VECS, BLOCK)
    joined = jnp.concatenate([own_blocks, sub_low, sub_high, region_low, region_high, far_blocks], axis=2)
    return joined.reshape(dev_count, TABLE, VECS, BLOCK)

def reference(test_vectors, weights, block_cols, block_count, halo_send, far_send):
    dev_count = N_REGION * N_SUB
    vectors = test_vectors.reshape(VECS, dev_count, BLK_DEV, BLOCK).transpose(1, 2, 0, 3)
    dev_weights = weights.reshape(dev_count, BLK_DEV, SLOTS, BLOCK, BLOCK)
    dev_cols = block_cols.reshape(dev_count, BLK_DEV, SLOTS)
    slot_ids = jnp.arange(SLOTS, dtype=jnp.int32)
    valid_slot = slot_ids[None, None, :] < block_count.reshape(dev_count, BLK_DEV)[:, :, None]

    def live_of(held, valid_one):
        return jnp.where(valid_one[:, :, None, None], held.astype(jnp.float32), jnp.float32(0.0))

    def degree_of(packed):
        held, valid_one = packed
        return lax.optimization_barrier(jnp.sum(live_of(held, valid_one), axis=(1, 3)))
    degree = lax.map(degree_of, (dev_weights, valid_slot))

    def product(packed):
        held, valid_one, cols_one, table_one = packed
        gathered = table_one[cols_one].astype(jnp.float32)
        return jnp.einsum('rsab,rsvb->rva', live_of(held, valid_one), gathered, precision=lax.Precision.HIGHEST)
    for sweep_index in range(SWEEPS):
        block_table = build_table(vectors.astype(jnp.bfloat16), halo_send, far_send)
        applied = lax.map(product, (dev_weights, valid_slot, dev_cols, block_table))
        vectors = (1.0 - damping) * vectors + damping * applied / degree[:, :, None, :]
    norm_total = lax.optimization_barrier(jnp.sum(vectors * vectors, axis=(0, 1, 3)))
    normal_vecs = (vectors / jnp.sqrt(norm_total / (dev_count * BLK_DEV * BLOCK))[None, None, :, None]).astype(jnp.bfloat16)
    block_table = build_table(normal_vecs, halo_send, far_send)

    def affine(packed):
        held, valid_one, cols_one, own_vecs, table_one = packed
        gathered = table_one[cols_one].astype(jnp.float32)
        own_float = own_vecs.astype(jnp.float32)
        cross_terms = jnp.einsum('rva,rsvb->rsab', own_float, gathered, precision=lax.Precision.HIGHEST)
        own_sq = lax.optimization_barrier(jnp.sum(own_float * own_float, axis=1))
        far_sq = lax.optimization_barrier(jnp.sum(gathered * gathered, axis=2))
        distance = (own_sq[:, None, :, None] + far_sq[:, :, None, :] - 2.0 * cross_terms) / VECS
        return (live_of(held, valid_one) / (1.0 + distance)).astype(jnp.bfloat16)
    affinity = lax.map(affine, (dev_weights, valid_slot, dev_cols, normal_vecs, block_table))
    affinity = affinity.reshape(NBLK, SLOTS, BLOCK, BLOCK)
    smoothed = normal_vecs.transpose(2, 0, 1, 3).reshape(VECS, NODES)
    return (smoothed, affinity)
```

```python
import functools

import jax
import jax.numpy as jnp
from jax import lax
from jax.experimental import pallas as pl
from jax.experimental.pallas import tpu as pltpu
from jax.sharding import PartitionSpec as P

SWEEPS = 3
MIN_LIVE = 5
EXTRA = 16

damping = 2.0 / 3.0

f32 = jnp.float32
bf16 = jnp.bfloat16
MESH = pl.DeviceIdType.MESH


def relax_kernel(
    n_region,
    n_sub,
    cols_ref,
    count_ref,
    halo_ref,
    far_ref,
    start_ref,
    weights_hbm,
    own_out,
    table_out,
    wts,
    vec,
    scale,
    own,
    marks,
    part_sub,
    part_region,
    *rest,
):
    tables, sends = rest[: SWEEPS + 1], rest[SWEEPS + 1 : 2 * SWEEPS + 2]
    wts_sem, send_sem, recv_sem, norm_send_sem, norm_recv_sem = rest[2 * SWEEPS + 2 :]
    rows, slots, size = wts.shape[:3]
    vecs = vec.shape[1]
    halo = halo_ref.shape[2]
    far = far_ref.shape[2]
    zero_at = tables[0].shape[0] - 1
    far_at = rows + 4 * halo
    me_sub, me_region = lax.axis_index("sub"), lax.axis_index("region")

    barrier = pltpu.get_barrier_semaphore()
    for axis, me, count in (("sub", me_sub, n_sub), ("region", me_region, n_region)):
        for j in range(1, count):
            pl.semaphore_signal(
                barrier, inc=1, device_id={axis: lax.rem(me + j, count)}, device_id_type=MESH
            )

    chunks = wts_sem.shape[0]
    per = rows // chunks
    loads = []
    for c in range(chunks):
        span = pl.ds(c * per, per)
        load = pltpu.make_async_copy(weights_hbm.at[span], wts.at[span], wts_sem.at[c])
        load.start()
        loads.append(load)

    marks[0] = jnp.ones((vecs, size), bf16)
    marks[1] = jnp.zeros((vecs, size), bf16)
    for table in tables:
        table[zero_at] = jnp.zeros((vecs, size), bf16)
    for r in range(rows):
        rounded = start_ref[:, r * size : (r + 1) * size].astype(bf16)
        own[r] = rounded
        tables[0][r] = rounded

    def exchange(k):
        table, send = tables[k], sends[k]
        copies = []
        faces = ((2, "region", me_region, n_region, 1), (3, "region", me_region, n_region, -1),
                 (0, "sub", me_sub, n_sub, 1), (1, "sub", me_sub, n_sub, -1))
        for face, axis, me, count, step in faces:
            def pick(i, carry):
                send[face * halo + i] = own[halo_ref[0, face, i]]
                return carry
            lax.fori_loop(0, halo, pick, 0, unroll=True)
            copy = pltpu.make_async_remote_copy(
                src_ref=send.at[pl.ds(face * halo, halo)],
                dst_ref=table.at[pl.ds(rows + face * halo, halo)],
                send_sem=send_sem.at[k, face],
                recv_sem=recv_sem.at[k, face],
                device_id={axis: lax.rem(me + step + count, count)},
                device_id_type=MESH,
            )
            copy.start()
            copies.append(copy)
        for j in range(1, n_sub):
            to = lax.rem(me_sub + j, n_sub)
            base = 4 * halo + (j - 1) * far
            for i in range(far):
                send[base + i] = own[far_ref[0, to, i]]
            copy = pltpu.make_async_remote_copy(
                src_ref=send.at[pl.ds(base, far)],
                dst_ref=table.at[pl.ds(far_at + me_sub * far, far)],
                send_sem=send_sem.at[k, 3 + j],
                recv_sem=recv_sem.at[k, 3 + j],
                device_id={"sub": to},
                device_id_type=MESH,
            )
            copy.start()
            copies.append(copy)
        for i in range(far):
            table[far_at + me_sub * far + i] = own[far_ref[0, me_sub, i]]
        return copies

    def sweep(k, first_row, row_count, total):
        table = tables[k]

        def one_row(r, total):
            live = [s < count_ref[r] for s in range(slots)]
            where = [jnp.where(live[s], cols_ref[r, s], zero_at) for s in range(slots)]
            left = jnp.concatenate([table[where[s]] for s in range(slots)], axis=1)
            if k == 0:
                ones = [marks[jnp.where(live[s], 0, 1)] for s in range(slots)]
                left = jnp.concatenate([left, jnp.concatenate(ones, axis=1)], axis=0)
            right = jnp.concatenate([wts[r, s] for s in range(slots)], axis=1)
            applied = lax.dot_general(
                left, right, (((1,), (1,)), ((), ())), preferred_element_type=f32
            )
            if k == 0:
                weight = damping / applied[vecs:]
                scale[r] = weight
                applied = applied[:vecs]
                held = start_ref[:, pl.ds(pl.multiple_of(r * size, size), size)]
            else:
                weight = scale[r]
                held = vec[r]
            moved = (1.0 - damping) * held + applied * weight
            vec[r] = moved
            rounded = moved.astype(bf16)
            own[r] = rounded
            if k + 1 < SWEEPS:
                tables[k + 1][r] = rounded
                return total
            return total + moved * moved

        return lax.fori_loop(first_row, first_row + row_count, one_row, total, unroll=2)

    pl.semaphore_wait(barrier, n_sub + n_region - 2)
    started = []
    total = jnp.zeros((vecs, size), f32)
    for k in range(SWEEPS):
        copies = exchange(k)
        started += copies
        for copy in copies:
            copy.wait_recv()
        if k == 0:
            for c in range(chunks):
                loads[c].wait()
                sweep(k, c * per, per, jnp.zeros((vecs, size), f32))
        else:
            total = sweep(k, 0, rows, jnp.zeros((vecs, size), f32))

    def share(part, value, axis, me, count, first_sem):
        part[me] = value
        copies = []
        for j in range(1, count):
            copy = pltpu.make_async_remote_copy(
                src_ref=part.at[me],
                dst_ref=part.at[me],
                send_sem=norm_send_sem.at[first_sem + j],
                recv_sem=norm_recv_sem.at[first_sem + j],
                device_id={axis: lax.rem(me + j, count)},
                device_id_type=MESH,
            )
            copy.start()
            copies.append(copy)
        return copies

    def added(part, copies):
        for copy in copies:
            copy.wait_recv()
        value = part[0]
        for q in range(1, part.shape[0]):
            value = value + part[q]
        return value

    norm_sub = share(part_sub, total, "sub", me_sub, n_sub, 0)
    copies = exchange(SWEEPS)
    started += copies
    sub_total = added(part_sub, norm_sub)
    norm_region = share(part_region, sub_total, "region", me_region, n_region, n_sub)
    full = added(part_region, norm_region)
    norm_total = jnp.sum(full, axis=1, keepdims=True)
    nodes = rows * size * n_region * n_sub
    factor = jnp.broadcast_to(1.0 / jnp.sqrt(norm_total / nodes), (vecs, size))
    row_id = lax.broadcasted_iota(jnp.int32, (EXTRA, size), 0)

    def pieces(value):
        top = value.astype(bf16).astype(f32)
        middle = (value - top).astype(bf16).astype(f32)
        return top, middle, value - top - middle

    def squares(values):
        held = values.astype(f32)
        return jnp.sum(held * held, axis=0, keepdims=True) * (1.0 / vecs)

    def far_form(values):
        top, middle, low = pieces(squares(values))
        extra = jnp.where(row_id == 0, top, jnp.where(row_id == 1, middle, jnp.where(
            row_id == 2, low, jnp.where(row_id < 6, 1.0, 0.0))))
        return extra.astype(bf16)

    def own_form(values):
        top, middle, low = pieces(squares(values) + 1.0)
        extra = jnp.where(row_id == 3, top, jnp.where(row_id == 4, middle, jnp.where(
            row_id == 5, low, jnp.where(row_id < 3, 1.0, 0.0))))
        return extra.astype(bf16)

    def own_row(r, carry):
        values = (vec[r] * factor).astype(bf16)
        own_out[r, 0:vecs] = values * (-2.0 / vecs)
        own_out[r, vecs : vecs + EXTRA] = own_form(values)
        table_out[r, 0:vecs] = values
        table_out[r, vecs : vecs + EXTRA] = far_form(values)
        return carry

    lax.fori_loop(0, rows, own_row, 0, unroll=2)
    for copy in copies:
        copy.wait_recv()

    def far_row(p, carry):
        values = (tables[SWEEPS][p].astype(f32) * factor).astype(bf16)
        table_out[p, 0:vecs] = values
        table_out[p, vecs : vecs + EXTRA] = far_form(values)
        return carry

    lax.fori_loop(rows, zero_at, far_row, 0, unroll=2)
    for copy in started + norm_sub + norm_region:
        copy.wait_send()


def affinity_kernel(cols_ref, count_ref, own_ref, table_ref, wts_ref, smoothed_ref, aff_ref):
    per, slots, size = wts_ref.shape[:3]
    vecs = smoothed_ref.shape[0]
    step = pl.program_id(0)

    for i in range(per):
        r = step * per + i
        near = own_ref[i]
        smoothed_ref[:, i * size : (i + 1) * size] = table_ref[r, 0:vecs]
        far = jnp.concatenate([table_ref[cols_ref[r, s]] for s in range(slots)], axis=1)
        below = lax.dot_general(
            near, far, (((0,), (0,)), ((), ())), preferred_element_type=f32
        )
        for s in range(slots):
            ratio = pl.reciprocal(below[:, s * size : (s + 1) * size], approx=True)
            value = wts_ref[i, s].astype(f32) * ratio
            if s >= MIN_LIVE:
                value = jnp.where(s < count_ref[r], value, 0.0)
            aff_ref[i, s] = value.astype(bf16)


def local(n_region, n_sub, test_vectors, weights, block_cols, block_count, halo_send, far_send):
    vecs = test_vectors.shape[0]
    rows, slots, size, _ = weights.shape
    halo, far = halo_send.shape[2], far_send.shape[2]
    table = rows + 4 * halo + n_sub * far
    block = (vecs, size)
    smem = pl.BlockSpec(memory_space=pltpu.SMEM)
    vmem = pl.BlockSpec(memory_space=pltpu.VMEM)
    chunks = 8
    own_blocks, table_blocks = pl.pallas_call(
        functools.partial(relax_kernel, n_region, n_sub),
        out_shape=(
            jax.ShapeDtypeStruct((rows, vecs + EXTRA, size), bf16),
            jax.ShapeDtypeStruct((table, vecs + EXTRA, size), bf16),
        ),
        in_specs=[smem, smem, smem, smem, vmem, pl.BlockSpec(memory_space=pl.ANY)],
        out_specs=(vmem, vmem),
        scratch_shapes=[
            pltpu.VMEM(weights.shape, bf16),
            pltpu.VMEM((rows,) + block, f32),
            pltpu.VMEM((rows,) + block, f32),
            pltpu.VMEM((rows,) + block, bf16),
            pltpu.VMEM((2,) + block, bf16),
            pltpu.VMEM((n_sub,) + block, f32),
            pltpu.VMEM((n_region,) + block, f32),
        ]
        + [pltpu.VMEM((table + 1,) + block, bf16)] * (SWEEPS + 1)
        + [pltpu.VMEM((4 * halo + (n_sub - 1) * far,) + block, bf16)] * (SWEEPS + 1)
        + [
            pltpu.SemaphoreType.DMA((chunks,)),
            pltpu.SemaphoreType.DMA((SWEEPS + 1, 3 + n_sub)),
            pltpu.SemaphoreType.DMA((SWEEPS + 1, 3 + n_sub)),
            pltpu.SemaphoreType.DMA((n_sub + n_region,)),
            pltpu.SemaphoreType.DMA((n_sub + n_region,)),
        ],
        compiler_params=pltpu.CompilerParams(
            collective_id=0, has_side_effects=True, vmem_limit_bytes=40 * 1024 * 1024
        ),
        name="relax",
    )(block_cols, block_count, halo_send, far_send, test_vectors, weights)

    per = 4
    smoothed, affinity = pl.pallas_call(
        affinity_kernel,
        out_shape=(
            jax.ShapeDtypeStruct((vecs, rows * size), bf16),
            jax.ShapeDtypeStruct(weights.shape, bf16),
        ),
        grid=(rows // per,),
        in_specs=[
            smem,
            smem,
            pl.BlockSpec((per, vecs + EXTRA, size), lambda i: (i, 0, 0)),
            pl.BlockSpec((table, vecs + EXTRA, size), lambda i: (0, 0, 0)),
            pl.BlockSpec((per, slots, size, size), lambda i: (i, 0, 0, 0)),
        ],
        out_specs=(
            pl.BlockSpec((vecs, per * size), lambda i: (0, i)),
            pl.BlockSpec((per, slots, size, size), lambda i: (i, 0, 0, 0)),
        ),
        compiler_params=pltpu.CompilerParams(vmem_limit_bytes=32 * 1024 * 1024),
        name="affinity",
    )(block_cols, block_count, own_blocks, table_blocks, weights)
    return smoothed, affinity


def solution(mesh):
    return jax.shard_map(
        functools.partial(local, mesh.shape["region"], mesh.shape["sub"]),
        mesh=mesh,
        in_specs=(
            P(None, ("region", "sub")),
            P(("region", "sub"), None, None, None),
            P(("region", "sub"), None),
            P(("region", "sub")),
            P(("region", "sub"), None, None),
            P(("region", "sub"), None, None),
        ),
        out_specs=(P(None, ("region", "sub")), P(("region", "sub"), None, None, None)),
        check_vma=False,
    )
```

```python
import functools

import jax
import jax.numpy as jnp
from jax import lax
from jax.experimental import pallas as pl
from jax.experimental.pallas import tpu as pltpu
from jax.sharding import PartitionSpec as P

SWEEPS = 3
MIN_LIVE = 5
EXTRA = 16

damping = 2.0 / 3.0

f32 = jnp.float32
bf16 = jnp.bfloat16
MESH = pl.DeviceIdType.MESH


def relax_kernel(
    n_region,
    n_sub,
    cols_hbm,
    count_hbm,
    halo_hbm,
    far_hbm,
    start_hbm,
    weights_hbm,
    own_out,
    table_out,
    cols_ref,
    count_ref,
    halo_ref,
    far_ref,
    start_ref,
    wts,
    turned,
    vec,
    scale,
    own,
    marks,
    part_sub,
    part_region,
    *rest,
):
    tables, sends = rest[: SWEEPS + 1], rest[SWEEPS + 1 : 2 * SWEEPS + 2]
    list_sem, wts_sem, send_sem, recv_sem, norm_send_sem, norm_recv_sem = rest[2 * SWEEPS + 2 :]
    rows, slots, size = wts.shape[:3]
    vecs = vec.shape[1]
    halo = halo_ref.shape[2]
    far = far_ref.shape[1]
    zero_at = tables[0].shape[0] - 1
    far_at = rows + 4 * halo
    me_sub, me_region = lax.axis_index("sub"), lax.axis_index("region")

    barrier = pltpu.get_barrier_semaphore()
    for axis, me, count in (("sub", me_sub, n_sub), ("region", me_region, n_region)):
        for j in range(1, count):
            pl.semaphore_signal(
                barrier, inc=1, device_id={axis: lax.rem(me + j, count)}, device_id_type=MESH
            )

    small = ((start_hbm, start_ref), (halo_hbm, halo_ref), (far_hbm, far_ref),
             (cols_hbm, cols_ref), (count_hbm, count_ref))
    lists = [
        pltpu.make_async_copy(source, target, list_sem.at[i])
        for i, (source, target) in enumerate(small)
    ]
    for load in lists:
        load.start()
    chunks = wts_sem.shape[0]
    per = rows // chunks
    loads = []
    for c in range(chunks):
        span = pl.ds(c * per, per)
        load = pltpu.make_async_copy(weights_hbm.at[span], wts.at[span], wts_sem.at[c])
        load.start()
        loads.append(load)

    marks[0] = jnp.ones((vecs, size), bf16)
    marks[1] = jnp.zeros((vecs, size), bf16)
    for table in tables:
        table[zero_at] = jnp.zeros((vecs, size), bf16)
    lists[0].wait()
    for r in range(rows):
        rounded = start_ref[:, r * size : (r + 1) * size].astype(bf16)
        own[r] = rounded
        tables[0][r] = rounded

    def exchange(k):
        table, send = tables[k], sends[k]
        copies = []
        faces = ((2, "region", me_region, n_region, 1), (3, "region", me_region, n_region, -1),
                 (0, "sub", me_sub, n_sub, 1), (1, "sub", me_sub, n_sub, -1))
        for face, axis, me, count, step in faces:
            def pick(i, carry):
                send[face * halo + i] = own[halo_ref[0, face, i]]
                return carry
            lax.fori_loop(0, halo, pick, 0, unroll=True)
            copy = pltpu.make_async_remote_copy(
                src_ref=send.at[pl.ds(face * halo, halo)],
                dst_ref=table.at[pl.ds(rows + face * halo, halo)],
                send_sem=send_sem.at[k, face],
                recv_sem=recv_sem.at[k, face],
                device_id={axis: lax.rem(me + step + count, count)},
                device_id_type=MESH,
            )
            copy.start()
            copies.append(copy)
        for j in range(1, n_sub):
            to = lax.rem(me_sub + j, n_sub)
            base = 4 * halo + (j - 1) * far
            for i in range(far):
                send[base + i] = own[far_ref[0, i, to]]
            copy = pltpu.make_async_remote_copy(
                src_ref=send.at[pl.ds(base, far)],
                dst_ref=table.at[pl.ds(far_at + me_sub * far, far)],
                send_sem=send_sem.at[k, 3 + j],
                recv_sem=recv_sem.at[k, 3 + j],
                device_id={"sub": to},
                device_id_type=MESH,
            )
            copy.start()
            copies.append(copy)
        for i in range(far):
            table[far_at + me_sub * far + i] = own[far_ref[0, i, me_sub]]
        return copies

    def turn(r, carry):
        ones = [marks[jnp.where(s < count_ref[r], 0, 1)] for s in range(slots)]
        columns = jnp.concatenate([wts[r, s].T for s in range(slots)], axis=0)
        turned[r] = columns
        degree = lax.dot_general(
            jnp.concatenate(ones, axis=1),
            columns,
            (((1,), (0,)), ((), ())),
            preferred_element_type=f32,
        )
        scale[r] = damping / degree
        return carry

    def sweep(k, total):
        table = tables[k]

        def one_row(r, total):
            live = [s < count_ref[r] for s in range(slots)]
            where = [jnp.where(live[s], cols_ref[s, r], zero_at) for s in range(slots)]
            left = jnp.concatenate([table[where[s]] for s in range(slots)], axis=1)
            applied = lax.dot_general(
                left, turned[r], (((1,), (0,)), ((), ())), preferred_element_type=f32
            )
            if k == 0:
                held = start_ref[:, pl.ds(pl.multiple_of(r * size, size), size)]
            else:
                held = vec[r]
            moved = (1.0 - damping) * held + applied * scale[r]
            vec[r] = moved
            rounded = moved.astype(bf16)
            own[r] = rounded
            if k + 1 < SWEEPS:
                tables[k + 1][r] = rounded
                return total
            return total + moved * moved

        return lax.fori_loop(0, rows, one_row, total, unroll=8)

    for load in lists[1:]:
        load.wait()
    pl.semaphore_wait(barrier, n_sub + n_region - 2)
    started = []
    total = jnp.zeros((vecs, size), f32)
    for k in range(SWEEPS):
        copies = exchange(k)
        started += copies
        if k == 0:
            for c in range(chunks):
                loads[c].wait()
                lax.fori_loop(c * per, (c + 1) * per, turn, 0, unroll=True)
        for copy in copies:
            copy.wait_recv()
        total = sweep(k, jnp.zeros((vecs, size), f32))

    def share(part, value, axis, me, count, first_sem):
        part[me] = value
        copies = []
        for j in range(1, count):
            copy = pltpu.make_async_remote_copy(
                src_ref=part.at[me],
                dst_ref=part.at[me],
                send_sem=norm_send_sem.at[first_sem + j],
                recv_sem=norm_recv_sem.at[first_sem + j],
                device_id={axis: lax.rem(me + j, count)},
                device_id_type=MESH,
            )
            copy.start()
            copies.append(copy)
        return copies

    def added(part, copies):
        for copy in copies:
            copy.wait_recv()
        value = part[0]
        for q in range(1, part.shape[0]):
            value = value + part[q]
        return value

    norm_sub = share(part_sub, total, "sub", me_sub, n_sub, 0)
    copies = exchange(SWEEPS)
    started += copies
    sub_total = added(part_sub, norm_sub)
    norm_region = share(part_region, sub_total, "region", me_region, n_region, n_sub)
    full = added(part_region, norm_region)
    norm_total = jnp.sum(full, axis=1, keepdims=True)
    nodes = rows * size * n_region * n_sub
    factor = jnp.broadcast_to(1.0 / jnp.sqrt(norm_total / nodes), (vecs, size))
    row_id = lax.broadcasted_iota(jnp.int32, (EXTRA, size), 0)

    def pieces(value):
        top = value.astype(bf16).astype(f32)
        middle = (value - top).astype(bf16).astype(f32)
        return top, middle, value - top - middle

    def squares(values):
        held = values.astype(f32)
        return jnp.sum(held * held, axis=0, keepdims=True) * (1.0 / vecs)

    def far_form(values):
        top, middle, low = pieces(squares(values))
        extra = jnp.where(row_id == 0, top, jnp.where(row_id == 1, middle, jnp.where(
            row_id == 2, low, jnp.where(row_id < 6, 1.0, 0.0))))
        return extra.astype(bf16)

    def own_form(values):
        top, middle, low = pieces(squares(values) + 1.0)
        extra = jnp.where(row_id == 3, top, jnp.where(row_id == 4, middle, jnp.where(
            row_id == 5, low, jnp.where(row_id < 3, 1.0, 0.0))))
        return extra.astype(bf16)

    def own_row(r, carry):
        values = (vec[r] * factor).astype(bf16)
        own_out[r, 0:vecs] = values * (-2.0 / vecs)
        own_out[r, vecs : vecs + EXTRA] = own_form(values)
        table_out[r, 0:vecs] = values
        table_out[r, vecs : vecs + EXTRA] = far_form(values)
        return carry

    lax.fori_loop(0, rows, own_row, 0, unroll=4)
    for copy in copies:
        copy.wait_recv()

    def far_row(p, carry):
        values = (tables[SWEEPS][p].astype(f32) * factor).astype(bf16)
        table_out[p, 0:vecs] = values
        table_out[p, vecs : vecs + EXTRA] = far_form(values)
        return carry

    lax.fori_loop(rows, zero_at, far_row, 0, unroll=8)
    for copy in started + norm_sub + norm_region:
        copy.wait_send()


def affinity_kernel(cols_ref, count_ref, own_ref, table_ref, wts_ref, smoothed_ref, aff_ref):
    per, slots, size = aff_ref.shape[:3]
    vecs = smoothed_ref.shape[0]
    step = pl.program_id(0)

    for i in range(per):
        r = step * per + i
        near = own_ref[r]
        smoothed_ref[:, i * size : (i + 1) * size] = table_ref[r, 0:vecs]
        far = jnp.concatenate([table_ref[cols_ref[s, r]] for s in range(slots)], axis=1)
        below = lax.dot_general(
            near, far, (((0,), (0,)), ((), ())), preferred_element_type=f32
        )
        for s in range(slots):
            ratio = pl.reciprocal(below[:, s * size : (s + 1) * size], approx=True)
            value = wts_ref[r, s].astype(f32) * ratio
            if s >= MIN_LIVE:
                value = jnp.where(s < count_ref[r], value, 0.0)
            aff_ref[i, s] = value.astype(bf16)


def local(n_region, n_sub, test_vectors, weights, block_cols, block_count, halo_send, far_send):
    vecs = test_vectors.shape[0]
    rows, slots, size, _ = weights.shape
    halo, far = halo_send.shape[2], far_send.shape[2]
    table = rows + 4 * halo + n_sub * far
    block = (vecs, size)
    smem = pl.BlockSpec(memory_space=pltpu.SMEM)
    vmem = pl.BlockSpec(memory_space=pltpu.VMEM)
    chunks = 8
    cols = block_cols.T
    far_lists = far_send.transpose(0, 2, 1)
    own_blocks, table_blocks = pl.pallas_call(
        functools.partial(relax_kernel, n_region, n_sub),
        out_shape=(
            jax.ShapeDtypeStruct((rows, vecs + EXTRA, size), bf16),
            jax.ShapeDtypeStruct((table, vecs + EXTRA, size), bf16),
        ),
        in_specs=[pl.BlockSpec(memory_space=pltpu.HBM)] * 6,
        out_specs=(vmem, vmem),
        scratch_shapes=[
            pltpu.SMEM(cols.shape, jnp.int32),
            pltpu.SMEM(block_count.shape, jnp.int32),
            pltpu.SMEM(halo_send.shape, jnp.int32),
            pltpu.SMEM(far_lists.shape, jnp.int32),
            pltpu.VMEM(test_vectors.shape, f32),
            pltpu.VMEM(weights.shape, bf16),
            pltpu.VMEM((rows, slots * size, size), bf16),
            pltpu.VMEM((rows,) + block, f32),
            pltpu.VMEM((rows,) + block, f32),
            pltpu.VMEM((rows,) + block, bf16),
            pltpu.VMEM((2,) + block, bf16),
            pltpu.VMEM((n_sub,) + block, f32),
            pltpu.VMEM((n_region,) + block, f32),
        ]
        + [pltpu.VMEM((table + 1,) + block, bf16)] * (SWEEPS + 1)
        + [pltpu.VMEM((4 * halo + (n_sub - 1) * far,) + block, bf16)] * (SWEEPS + 1)
        + [
            pltpu.SemaphoreType.DMA((5,)),
            pltpu.SemaphoreType.DMA((chunks,)),
            pltpu.SemaphoreType.DMA((SWEEPS + 1, 3 + n_sub)),
            pltpu.SemaphoreType.DMA((SWEEPS + 1, 3 + n_sub)),
            pltpu.SemaphoreType.DMA((n_sub + n_region,)),
            pltpu.SemaphoreType.DMA((n_sub + n_region,)),
        ],
        compiler_params=pltpu.CompilerParams(
            collective_id=0, has_side_effects=True, vmem_limit_bytes=40 * 1024 * 1024
        ),
        name="relax",
    )(*[pltpu.with_memory_space_constraint(x, pltpu.HBM) for x in (cols, block_count, halo_send, far_lists, test_vectors, weights)])

    per = 4
    smoothed, affinity = pl.pallas_call(
        affinity_kernel,
        out_shape=(
            jax.ShapeDtypeStruct((vecs, rows * size), bf16),
            jax.ShapeDtypeStruct(weights.shape, bf16),
        ),
        grid=(rows // per,),
        in_specs=[
            smem,
            smem,
            vmem,
            vmem,
            vmem,
        ],
        out_specs=(
            pl.BlockSpec((vecs, per * size), lambda i: (0, i)),
            pl.BlockSpec((per, slots, size, size), lambda i: (i, 0, 0, 0)),
        ),
        compiler_params=pltpu.CompilerParams(vmem_limit_bytes=32 * 1024 * 1024),
        name="affinity",
    )(cols, block_count, own_blocks, table_blocks, weights)
    return smoothed, affinity


def solution(mesh):
    return jax.shard_map(
        functools.partial(local, mesh.shape["region"], mesh.shape["sub"]),
        mesh=mesh,
        in_specs=(
            P(None, ("region", "sub")),
            P(("region", "sub"), None, None, None),
            P(("region", "sub"), None),
            P(("region", "sub")),
            P(("region", "sub"), None, None),
            P(("region", "sub"), None, None),
        ),
        out_specs=(P(None, ("region", "sub")), P(("region", "sub"), None, None, None)),
        check_vma=False,
    )
```

```python
import functools

import jax
import jax.numpy as jnp
from jax import lax
from jax.experimental import pallas as pl
from jax.experimental.pallas import tpu as pltpu
from jax.sharding import PartitionSpec as P

SWEEPS = 3
MIN_LIVE = 5
EXTRA = 16

damping = 2.0 / 3.0

f32 = jnp.float32
bf16 = jnp.bfloat16
MESH = pl.DeviceIdType.MESH


def relax_kernel(
    n_region,
    n_sub,
    cols_hbm,
    count_hbm,
    halo_hbm,
    far_hbm,
    start_hbm,
    weights_hbm,
    own_out,
    table_out,
    cols_ref,
    count_ref,
    halo_ref,
    far_ref,
    start_ref,
    wts,
    turned,
    vec,
    scale,
    own,
    marks,
    part_sub,
    part_region,
    *rest,
):
    tables, sends = rest[: SWEEPS + 1], rest[SWEEPS + 1 : 2 * SWEEPS + 2]
    list_sem, wts_sem, send_sem, recv_sem, norm_send_sem, norm_recv_sem = rest[2 * SWEEPS + 2 :]
    rows, slots, size = wts.shape[:3]
    vecs = vec.shape[1]
    halo = halo_ref.shape[2]
    far = far_ref.shape[1]
    zero_at = tables[0].shape[0] - 1
    far_at = rows + 4 * halo
    me_sub, me_region = lax.axis_index("sub"), lax.axis_index("region")

    barrier = pltpu.get_barrier_semaphore()
    for axis, me, count in (("sub", me_sub, n_sub), ("region", me_region, n_region)):
        for j in range(1, count):
            pl.semaphore_signal(
                barrier, inc=1, device_id={axis: lax.rem(me + j, count)}, device_id_type=MESH
            )

    small = ((start_hbm, start_ref), (halo_hbm, halo_ref), (far_hbm, far_ref),
             (cols_hbm, cols_ref), (count_hbm, count_ref))
    lists = [
        pltpu.make_async_copy(source, target, list_sem.at[i])
        for i, (source, target) in enumerate(small)
    ]
    for load in lists:
        load.start()
    chunks = wts_sem.shape[0]
    per = rows // chunks
    loads = []
    for c in range(chunks):
        span = pl.ds(c * per, per)
        load = pltpu.make_async_copy(weights_hbm.at[span], wts.at[span], wts_sem.at[c])
        load.start()
        loads.append(load)

    marks[0] = jnp.ones((vecs, size), bf16)
    marks[1] = jnp.zeros((vecs, size), bf16)
    for table in tables:
        table[zero_at] = jnp.zeros((vecs, size), bf16)
    lists[0].wait()
    for r in range(rows):
        rounded = start_ref[:, r * size : (r + 1) * size].astype(bf16)
        own[r] = rounded
        tables[0][r] = rounded

    def exchange(k):
        table, send = tables[k], sends[k]
        copies = []
        faces = ((2, "region", me_region, n_region, 1), (3, "region", me_region, n_region, -1),
                 (0, "sub", me_sub, n_sub, 1), (1, "sub", me_sub, n_sub, -1))
        for face, axis, me, count, step in faces:
            def pick(i, carry):
                send[face * halo + i] = own[halo_ref[0, face, i]]
                return carry
            lax.fori_loop(0, halo, pick, 0, unroll=True)
            copy = pltpu.make_async_remote_copy(
                src_ref=send.at[pl.ds(face * halo, halo)],
                dst_ref=table.at[pl.ds(rows + face * halo, halo)],
                send_sem=send_sem.at[k, face],
                recv_sem=recv_sem.at[k, face],
                device_id={axis: lax.rem(me + step + count, count)},
                device_id_type=MESH,
            )
            copy.start()
            copies.append(copy)
        for j in range(1, n_sub):
            to = lax.rem(me_sub + j, n_sub)
            base = 4 * halo + (j - 1) * far
            for i in range(far):
                send[base + i] = own[far_ref[0, i, to]]
            copy = pltpu.make_async_remote_copy(
                src_ref=send.at[pl.ds(base, far)],
                dst_ref=table.at[pl.ds(far_at + me_sub * far, far)],
                send_sem=send_sem.at[k, 3 + j],
                recv_sem=recv_sem.at[k, 3 + j],
                device_id={"sub": to},
                device_id_type=MESH,
            )
            copy.start()
            copies.append(copy)
        for i in range(far):
            table[far_at + me_sub * far + i] = own[far_ref[0, i, me_sub]]
        return copies

    def turn(r, carry):
        ones = [marks[jnp.where(s < count_ref[r], 0, 1)] for s in range(slots)]
        columns = jnp.concatenate([wts[r, s].T for s in range(slots)], axis=0)
        turned[r] = columns
        degree = lax.dot_general(
            jnp.concatenate(ones, axis=1),
            columns,
            (((1,), (0,)), ((), ())),
            preferred_element_type=f32,
        )
        scale[r] = damping / degree
        return carry

    def sweep(k, total):
        table = tables[k]

        def one_row(r, total):
            live = [s < count_ref[r] for s in range(slots)]
            where = [jnp.where(live[s], cols_ref[s, r], zero_at) for s in range(slots)]
            left = jnp.concatenate([table[where[s]] for s in range(slots)], axis=1)
            applied = lax.dot_general(
                left, turned[r], (((1,), (0,)), ((), ())), preferred_element_type=f32
            )
            if k == 0:
                held = start_ref[:, pl.ds(pl.multiple_of(r * size, size), size)]
            else:
                held = vec[r]
            moved = (1.0 - damping) * held + applied * scale[r]
            vec[r] = moved
            rounded = moved.astype(bf16)
            own[r] = rounded
            if k + 1 < SWEEPS:
                tables[k + 1][r] = rounded
                return total
            return total + moved * moved

        return lax.fori_loop(0, rows, one_row, total, unroll=16)

    for load in lists[1:]:
        load.wait()
    pl.semaphore_wait(barrier, n_sub + n_region - 2)
    started = []
    total = jnp.zeros((vecs, size), f32)
    for k in range(SWEEPS):
        copies = exchange(k)
        started += copies
        if k == 0:
            for c in range(chunks):
                loads[c].wait()
                lax.fori_loop(c * per, (c + 1) * per, turn, 0, unroll=True)
        for copy in copies:
            copy.wait_recv()
        total = sweep(k, jnp.zeros((vecs, size), f32))

    def share(part, value, axis, me, count, first_sem):
        part[me] = value
        copies = []
        for j in range(1, count):
            copy = pltpu.make_async_remote_copy(
                src_ref=part.at[me],
                dst_ref=part.at[me],
                send_sem=norm_send_sem.at[first_sem + j],
                recv_sem=norm_recv_sem.at[first_sem + j],
                device_id={axis: lax.rem(me + j, count)},
                device_id_type=MESH,
            )
            copy.start()
            copies.append(copy)
        return copies

    def added(part, copies):
        for copy in copies:
            copy.wait_recv()
        value = part[0]
        for q in range(1, part.shape[0]):
            value = value + part[q]
        return value

    norm_sub = share(part_sub, total, "sub", me_sub, n_sub, 0)
    copies = exchange(SWEEPS)
    started += copies
    sub_total = added(part_sub, norm_sub)
    norm_region = share(part_region, sub_total, "region", me_region, n_region, n_sub)
    full = added(part_region, norm_region)
    norm_total = jnp.sum(full, axis=1, keepdims=True)
    nodes = rows * size * n_region * n_sub
    factor = jnp.broadcast_to(1.0 / jnp.sqrt(norm_total / nodes), (vecs, size))
    row_id = lax.broadcasted_iota(jnp.int32, (EXTRA, size), 0)

    def pieces(value):
        top = value.astype(bf16).astype(f32)
        middle = (value - top).astype(bf16).astype(f32)
        return top, middle, value - top - middle

    def squares(values):
        held = values.astype(f32)
        return jnp.sum(held * held, axis=0, keepdims=True) * (1.0 / vecs)

    def far_form(values):
        top, middle, low = pieces(squares(values))
        extra = jnp.where(row_id == 0, top, jnp.where(row_id == 1, middle, jnp.where(
            row_id == 2, low, jnp.where(row_id < 6, 1.0, 0.0))))
        return extra.astype(bf16)

    def own_form(values):
        top, middle, low = pieces(squares(values) + 1.0)
        extra = jnp.where(row_id == 3, top, jnp.where(row_id == 4, middle, jnp.where(
            row_id == 5, low, jnp.where(row_id < 3, 1.0, 0.0))))
        return extra.astype(bf16)

    def own_row(r, carry):
        values = (vec[r] * factor).astype(bf16)
        own_out[r, 0:vecs] = values * (-2.0 / vecs)
        own_out[r, vecs : vecs + EXTRA] = own_form(values)
        table_out[r, 0:vecs] = values
        table_out[r, vecs : vecs + EXTRA] = far_form(values)
        return carry

    lax.fori_loop(0, rows, own_row, 0, unroll=4)
    for copy in copies:
        copy.wait_recv()

    def far_row(p, carry):
        values = (tables[SWEEPS][p].astype(f32) * factor).astype(bf16)
        table_out[p, 0:vecs] = values
        table_out[p, vecs : vecs + EXTRA] = far_form(values)
        return carry

    lax.fori_loop(rows, zero_at, far_row, 0, unroll=8)
    for copy in started + norm_sub + norm_region:
        copy.wait_send()


def affinity_kernel(
    cols_ref, count_ref, own_ref, table_ref, wts_ref, smoothed_ref, aff_hbm, held, sem
):
    rows, slots, size = wts_ref.shape[:3]
    vecs = smoothed_ref.shape[0]
    chunks = sem.shape[0]
    per = rows // chunks

    def copy_out(c):
        span = pl.ds(c * per, per)
        return pltpu.make_async_copy(held.at[span], aff_hbm.at[span], sem.at[c])

    def chunk(c, carry):
        for i in range(per):
            r = c * per + i
            near = own_ref[r]
            place = pl.ds(pl.multiple_of(r * size, size), size)
            smoothed_ref[:, place] = table_ref[r, 0:vecs]
            far = jnp.concatenate([table_ref[cols_ref[s, r]] for s in range(slots)], axis=1)
            below = lax.dot_general(
                near, far, (((0,), (0,)), ((), ())), preferred_element_type=f32
            )
            for s in range(slots):
                ratio = pl.reciprocal(below[:, s * size : (s + 1) * size], approx=True)
                value = wts_ref[r, s].astype(f32) * ratio
                if s >= MIN_LIVE:
                    value = jnp.where(s < count_ref[r], value, 0.0)
                held[r, s] = value.astype(bf16)
        copy_out(c).start()
        return carry

    [chunk(c, 0) for c in range(chunks)]

    def finish(c, carry):
        copy_out(c).wait()
        return carry

    lax.fori_loop(0, chunks, finish, 0)


def local(n_region, n_sub, test_vectors, weights, block_cols, block_count, halo_send, far_send):
    vecs = test_vectors.shape[0]
    rows, slots, size, _ = weights.shape
    halo, far = halo_send.shape[2], far_send.shape[2]
    table = rows + 4 * halo + n_sub * far
    block = (vecs, size)
    smem = pl.BlockSpec(memory_space=pltpu.SMEM)
    vmem = pl.BlockSpec(memory_space=pltpu.VMEM)
    chunks = 8
    cols = block_cols.T
    far_lists = far_send.transpose(0, 2, 1)
    own_blocks, table_blocks = pl.pallas_call(
        functools.partial(relax_kernel, n_region, n_sub),
        out_shape=(
            jax.ShapeDtypeStruct((rows, vecs + EXTRA, size), bf16),
            jax.ShapeDtypeStruct((table, vecs + EXTRA, size), bf16),
        ),
        in_specs=[pl.BlockSpec(memory_space=pltpu.HBM)] * 6,
        out_specs=(vmem, vmem),
        scratch_shapes=[
            pltpu.SMEM(cols.shape, jnp.int32),
            pltpu.SMEM(block_count.shape, jnp.int32),
            pltpu.SMEM(halo_send.shape, jnp.int32),
            pltpu.SMEM(far_lists.shape, jnp.int32),
            pltpu.VMEM(test_vectors.shape, f32),
            pltpu.VMEM(weights.shape, bf16),
            pltpu.VMEM((rows, slots * size, size), bf16),
            pltpu.VMEM((rows,) + block, f32),
            pltpu.VMEM((rows,) + block, f32),
            pltpu.VMEM((rows,) + block, bf16),
            pltpu.VMEM((2,) + block, bf16),
            pltpu.VMEM((n_sub,) + block, f32),
            pltpu.VMEM((n_region,) + block, f32),
        ]
        + [pltpu.VMEM((table + 1,) + block, bf16)] * (SWEEPS + 1)
        + [pltpu.VMEM((4 * halo + (n_sub - 1) * far,) + block, bf16)] * (SWEEPS + 1)
        + [
            pltpu.SemaphoreType.DMA((5,)),
            pltpu.SemaphoreType.DMA((chunks,)),
            pltpu.SemaphoreType.DMA((SWEEPS + 1, 3 + n_sub)),
            pltpu.SemaphoreType.DMA((SWEEPS + 1, 3 + n_sub)),
            pltpu.SemaphoreType.DMA((n_sub + n_region,)),
            pltpu.SemaphoreType.DMA((n_sub + n_region,)),
        ],
        compiler_params=pltpu.CompilerParams(
            collective_id=0, has_side_effects=True, vmem_limit_bytes=40 * 1024 * 1024
        ),
        name="relax",
    )(*[pltpu.with_memory_space_constraint(x, pltpu.HBM) for x in (cols, block_count, halo_send, far_lists, test_vectors, weights)])

    out_chunks = 16
    smoothed, affinity = pl.pallas_call(
        affinity_kernel,
        out_shape=(
            jax.ShapeDtypeStruct((vecs, rows * size), bf16),
            jax.ShapeDtypeStruct(weights.shape, bf16),
        ),
        in_specs=[
            smem,
            smem,
            vmem,
            vmem,
            vmem,
        ],
        out_specs=(
            vmem,
            pl.BlockSpec(memory_space=pltpu.HBM),
        ),
        scratch_shapes=[
            pltpu.VMEM(weights.shape, bf16),
            pltpu.SemaphoreType.DMA((out_chunks,)),
        ],
        compiler_params=pltpu.CompilerParams(vmem_limit_bytes=32 * 1024 * 1024),
        name="affinity",
    )(cols, block_count, own_blocks, table_blocks, weights)
    return smoothed, affinity


def solution(mesh):
    return jax.shard_map(
        functools.partial(local, mesh.shape["region"], mesh.shape["sub"]),
        mesh=mesh,
        in_specs=(
            P(None, ("region", "sub")),
            P(("region", "sub"), None, None, None),
            P(("region", "sub"), None),
            P(("region", "sub")),
            P(("region", "sub"), None, None),
            P(("region", "sub"), None, None),
        ),
        out_specs=(P(None, ("region", "sub")), P(("region", "sub"), None, None, None)),
        check_vma=False,
    )
```
